32 devices in a mesh: chan: 4 (over z), ctx: 8 (over y, x, core).
Axes of the slice: x: 2, y: 2, z: 4, core: 2. Of those that a mesh axis runs over, the one named last changes fastest.
Arguments:
- projected: bfloat16 [8, 512, 3, 4096], P('ctx', 'chan'), may hold values from -6 to 6
- short_taps: bfloat16 [3, 3, 4096], replicated, may hold values from -3 to 3
- long_filter: float32 [4096, 16], P('ctx', 'chan'), may hold values from -0.09375 to 0.09375
- skip_gain: float32 [4096], P('chan'), may hold values from -4 to 4
Outputs:
- gated: bfloat16 [4096, 4096], P('ctx', 'chan')
The draws below stay inside these ranges and needn't reach their ends.
All inputs are finite; a program needn't handle non-finite values.
Results may differ from the reference program's by a relative error of at most 0.0064.
Values may be sent and summed in bfloat16 or wider, within the bound.
A program may use at most 128 MiB of HBM per device.

```python
import jax
import jax.numpy as jnp
from jax import lax

DW = 4096
GROUP = 256
TAPS = 3
BLOCK = 512
LEN = 4096
GROUPS = 16
N_CTX = 8


def block_scale(rng, shape, shards, smallest, high):
    factor_of, own = 1.0, jax.random.fold_in(rng, 6)
    for position, parts in shards:
        draws = jnp.exp(jax.random.uniform(jax.random.fold_in(own, position), (parts,), jnp.float32, smallest / len(shards), high / len(shards)))
        factor_of = factor_of * jnp.repeat(draws, shape[position] // parts).reshape([-1 if axis == position else 1 for axis in range(len(shape))])
    return factor_of


def scatter_about(rng, dims, spread, bound, cuts=(), held_as=jnp.bfloat16):
    values = spread * jax.random.normal(rng, dims, jnp.float32)
    if cuts:
        values = values * block_scale(rng, dims, cuts, -0.22, 0.18)
    return jnp.clip(values, -bound, bound).astype(held_as)


def setup_inputs(seed: int = 0) -> dict:
    streams_of = jax.random.split(jax.random.key(seed), 5)
    projected = scatter_about(streams_of[0], (N_CTX, BLOCK, 3, DW), 1.0, 6.0, ((0, 8), (1, 4)))
    short_taps = scatter_about(streams_of[1], (TAPS, 3, DW), 0.6, 3.0)
    long_filter = scatter_about(streams_of[2], (LEN, GROUPS), LEN ** -0.5, 0.09375, ((0, 8), (1, 4)), jnp.float32)
    skip_gain = scatter_about(streams_of[3], (DW,), 1.0, 4.0, ((0, 4),), jnp.float32)
    return dict(projected=projected, short_taps=short_taps, long_filter=long_filter, skip_gain=skip_gain)


def stored(values):
    return lax.optimization_barrier(values.astype(jnp.bfloat16))


def reference(projected, short_taps, long_filter, skip_gain):
    flat = projected.reshape(LEN, 3, DW)

    def one_group(group_id):
        first_col = group_id * GROUP
        columns = lax.dynamic_slice_in_dim(flat, first_col, GROUP, 2).astype(jnp.float32)
        weights = lax.dynamic_slice_in_dim(short_taps, first_col, GROUP, 2).astype(jnp.float32)
        padded = jnp.pad(columns, ((TAPS - 1, 0), (0, 0), (0, 0)))
        summed = weights[0] * padded[TAPS - 1:TAPS - 1 + LEN]
        for offset in range(1, TAPS):
            summed = summed + weights[offset] * padded[TAPS - 1 - offset:TAPS - 1 - offset + LEN]
        queries = stored(summed[:, 0]).astype(jnp.float32)
        product = stored(summed[:, 1] * summed[:, 2]).astype(jnp.float32)
        kernel = lax.dynamic_index_in_dim(long_filter, group_id, 1, keepdims=False)
        spectrum = jnp.fft.rfft(product, n=2 * LEN, axis=0) * jnp.fft.rfft(kernel, n=2 * LEN)[:, None]
        convolved = jnp.fft.irfft(spectrum, n=2 * LEN, axis=0)[:LEN]
        gains = lax.dynamic_slice_in_dim(skip_gain, first_col, GROUP, 0)
        mixed = stored(convolved + gains * product).astype(jnp.float32)
        return (queries * mixed).astype(jnp.bfloat16)

    blocks = lax.map(one_group, jnp.arange(GROUPS, dtype=jnp.int32))
    return jnp.transpose(blocks, (1, 0, 2)).reshape(LEN, DW)
```

```python
import functools
import math

import jax
import jax.numpy as jnp
from jax import lax
from jax.experimental import pallas as pl
from jax.experimental.pallas import tpu as pltpu
from jax.sharding import PartitionSpec as P

TAPS = 3


PRECISE = lax.Precision.HIGHEST


def passed_along(value, axis, by):
    count = lax.axis_size(axis)
    pairs = [(i, i + by) for i in range(count) if 0 <= i + by < count]
    return lax.ppermute(value, axis, pairs)


def counting(length):
    return jnp.arange(length, dtype=jnp.int32)


def phases(first, second, length):
    turned = first[:, None] * second[None, :] % length
    angles = turned.astype(jnp.float32) * (2.0 * math.pi / length)
    return (jnp.cos(angles), jnp.sin(angles))


def rotate(real_part, imag_part, cosines, sines, direction):
    return (
        real_part * cosines - direction * imag_part * sines,
        imag_part * cosines + direction * real_part * sines,
    )


def complex_mix(pattern, cosines, sines, real_part, imag_part, direction):
    cos_real = jnp.einsum(pattern, cosines, real_part, precision=PRECISE)
    sin_real = jnp.einsum(pattern, sines, real_part, precision=PRECISE)
    if imag_part is None:
        return (cos_real, direction * sin_real)
    cos_imag = jnp.einsum(pattern, cosines, imag_part, precision=PRECISE)
    sin_imag = jnp.einsum(pattern, sines, imag_part, precision=PRECISE)
    return (cos_real - direction * sin_imag, cos_imag + direction * sin_real)


def leading_factor(length):
    chosen = 1
    for option in range(1, math.isqrt(length) + 1):
        if length % option == 0:
            chosen = option
    return chosen


def local_tables(first, second):
    cos_one, sin_one = phases(counting(first), counting(first), first)
    cos_two, sin_two = phases(counting(second), counting(second), second)
    cos_mid, sin_mid = phases(counting(first), counting(second), first * second)
    return (
        cos_one,
        sin_one,
        cos_two,
        sin_two,
        cos_mid[None, :, :, None],
        sin_mid[None, :, :, None],
    )


def inner_forward(real_part, imag_part):
    leading, length, columns = real_part.shape
    first = leading_factor(length)
    second = length // first
    cos_one, sin_one, cos_two, sin_two, cos_mid, sin_mid = local_tables(first, second)
    real_part = real_part.reshape(leading, first, second, columns)
    if imag_part is not None:
        imag_part = imag_part.reshape(leading, first, second, columns)
    real_part, imag_part = complex_mix(
        "bk,akjx->abjx", cos_one, sin_one, real_part, imag_part, -1.0
    )
    real_part, imag_part = rotate(real_part, imag_part, cos_mid, sin_mid, -1.0)
    return complex_mix("ej,abjx->abex", cos_two, sin_two, real_part, imag_part, -1.0)


def inner_inverse(real_part, imag_part):
    leading, first, second, columns = real_part.shape
    cos_one, sin_one, cos_two, sin_two, cos_mid, sin_mid = local_tables(first, second)
    real_part, imag_part = complex_mix("ej,abjx->abex", cos_two, sin_two, real_part, imag_part, 1.0)
    real_part, imag_part = rotate(real_part, imag_part, cos_mid, sin_mid, 1.0)
    real_part, imag_part = complex_mix("kb,abjx->akjx", cos_one, sin_one, real_part, imag_part, 1.0)
    return (
        real_part.reshape(leading, first * second, columns),
        imag_part.reshape(leading, first * second, columns),
    )


def featurize(earlier, own_rows, filter_taps):
    lag_rows = earlier.shape[0]
    length = own_rows.shape[0]
    extended = jnp.concatenate([earlier, own_rows], axis=0).astype(jnp.float32)
    weights = filter_taps.astype(jnp.float32)
    summed = weights[0] * extended[lag_rows : lag_rows + length]
    for offset in range(1, weights.shape[0]):
        summed = summed + weights[offset] * extended[lag_rows - offset : lag_rows - offset + length]
    queries = lax.optimization_barrier(summed[:, 0].astype(jnp.bfloat16))
    product = (summed[:, 1] * summed[:, 2]).astype(jnp.bfloat16)
    return (queries, product)


def whole_transform(real_part, imag_part):
    zeros = jnp.zeros_like(real_part)
    padded_real = jnp.concatenate([real_part, zeros], axis=0)[None]
    padded_imag = None
    if imag_part is not None:
        padded_imag = jnp.concatenate([imag_part, zeros], axis=0)[None]
    return inner_forward(padded_real, padded_imag)


def local_convolve(signal, filters, gains_here, position, per_group):
    length, columns = signal.shape
    groups_here = filters.shape[1]
    first_channel = position * columns
    pairs = signal.reshape(length, columns // 2, 2)
    real_in = pairs[:, :, 0]
    imag_in = pairs[:, :, 1]
    owners = (first_channel + 2 * counting(columns // 2)) // per_group
    selector = (counting(groups_here)[:, None] == owners[None, :]).astype(jnp.float32)
    filt_real, filt_imag = whole_transform(filters, None)
    filt_real = jnp.einsum("abex,xc->abec", filt_real, selector, precision=PRECISE)
    filt_imag = jnp.einsum("abex,xc->abec", filt_imag, selector, precision=PRECISE)
    sig_real, sig_imag = whole_transform(real_in, imag_in)
    prod_real = sig_real * filt_real - sig_imag * filt_imag
    prod_imag = sig_real * filt_imag + sig_imag * filt_real
    back_real, back_imag = inner_inverse(prod_real, prod_imag)
    inverse_scale = 1.0 / (2 * length)
    conv_real = back_real[0, :length] * inverse_scale
    conv_imag = back_imag[0, :length] * inverse_scale
    convolved = jnp.stack([conv_real, conv_imag], axis=2).reshape(length, columns)
    return convolved + gains_here * signal


def by_transform(projected, short_taps, long_filter, skip_gain):
    devices = lax.axis_size("ctx")
    position = lax.axis_index("ctx")
    channel_slot = lax.axis_index("chan")
    channels = skip_gain.shape[0]
    groups_here = long_filter.shape[1]
    per_group = channels // groups_here
    regrouped = lax.all_to_all(projected, "chan", split_axis=3, concat_axis=1, tiled=True)[0]
    taps_here = lax.dynamic_slice_in_dim(short_taps, channel_slot * channels, channels, 2)
    last_rows = regrouped[regrouped.shape[0] - (TAPS - 1) :]
    earlier = passed_along(last_rows, "ctx", 1)
    queries, product = featurize(earlier, regrouped, taps_here)
    kv_seq = lax.all_to_all(product[None], "ctx", split_axis=2, concat_axis=0, tiled=True)
    block_rows = kv_seq.shape[1]
    columns = kv_seq.shape[2]
    signal = kv_seq.reshape(devices * block_rows, columns).astype(jnp.float32)
    filters = lax.all_gather(long_filter, "ctx", axis=0, tiled=True)
    gains_here = lax.dynamic_slice_in_dim(skip_gain, position * columns, columns, 0)
    mixed = local_convolve(signal, filters, gains_here, position, per_group).astype(jnp.bfloat16)
    mixed = mixed.reshape(devices, block_rows, columns)
    mixed_rows = lax.all_to_all(mixed, "ctx", split_axis=0, concat_axis=2, tiled=True)[0]
    return (queries.astype(jnp.float32) * mixed_rows.astype(jnp.float32)).astype(jnp.bfloat16)


TILE = 256


def exchange_kernel(
    query_ref,
    kv_ref,
    lags_ref,
    gain_ref,
    out_ref,
    query_rows,
    kv_rows,
    kv_seq,
    mixed_out,
    mixed_in,
    toeplitz,
    kv_send,
    kv_recv,
    query_send,
    query_recv,
    seq_send,
    seq_recv,
    back_send,
    back_recv,
):
    chans = lax.axis_size("chan")
    blocks = lax.axis_size("ctx")
    my_chan = lax.axis_index("chan")
    my_block = lax.axis_index("ctx")
    rows = kv_ref.shape[0]
    width = kv_rows.shape[1]
    columns = kv_seq.shape[1]
    block_rows = rows * chans

    def other_chan(step):
        return lax.rem(my_chan + step + chans, chans)

    def other_block(step):
        return lax.rem(my_block + step + blocks, blocks)

    barrier = pltpu.get_barrier_semaphore()
    for step in range(1, chans):
        pl.semaphore_signal(barrier, inc=1, device_id={"chan": other_chan(step)})
    for step in range(1, blocks):
        pl.semaphore_signal(barrier, inc=1, device_id={"ctx": other_block(step)})
    pl.semaphore_wait(barrier, chans + blocks - 2)

    def lanes(index, size):
        return pl.ds(pl.multiple_of(index * size, size), size)

    def over_chan(source, target, send, recv, step):
        to = other_chan(step)
        return pltpu.make_async_remote_copy(
            src_ref=source.at[:, lanes(to, width)],
            dst_ref=target.at[lanes(my_chan, rows), :],
            send_sem=send.at[step],
            recv_sem=recv.at[step],
            device_id={"chan": to},
        )

    kv_copies = [over_chan(kv_ref, kv_rows, kv_send, kv_recv, step) for step in range(1, chans)]
    query_copies = [
        over_chan(query_ref, query_rows, query_send, query_recv, step) for step in range(1, chans)
    ]
    for copy in kv_copies:
        copy.start()
    kv_rows[lanes(my_chan, rows), :] = kv_ref[:, lanes(my_chan, width)]
    query_rows[lanes(my_chan, rows), :] = query_ref[:, lanes(my_chan, width)]

    seq_copies = []

    def forward(step):
        origin = other_chan(-step)
        here = lanes(origin, rows)
        there = lanes(my_block * chans + origin, rows)
        for hop in range(1, blocks):
            to = other_block(hop)
            copy = pltpu.make_async_remote_copy(
                src_ref=kv_rows.at[here, lanes(to, columns)],
                dst_ref=kv_seq.at[there, :],
                send_sem=seq_send.at[step, hop],
                recv_sem=seq_recv.at[step, hop],
                device_id={"ctx": to},
            )
            copy.start()
            seq_copies.append(copy)
        kv_seq[there, :] = kv_rows[here, lanes(my_block, columns)]

    forward(0)

    toeplitz[0:TILE, :] = jnp.zeros((TILE, TILE), jnp.bfloat16)
    length = kv_seq.shape[0]
    for tile in range(length // TILE):
        first = length - TILE - tile * TILE
        window = jnp.broadcast_to(lags_ref[:, first : first + 2 * TILE], (TILE, 2 * TILE))
        turned = pltpu.roll(window, TILE + 1, 1, stride=1, stride_axis=0)
        toeplitz[(tile + 1) * TILE : (tile + 2) * TILE, :] = turned[:, :TILE].astype(jnp.bfloat16)

    for step in range(1, chans):
        kv_copies[step - 1].wait_recv()
        forward(step)
    for copy in query_copies:
        copy.start()
    for copy in seq_copies:
        copy.wait_recv()

    gain = gain_ref[...]

    def returning(hop):
        to = other_block(hop)
        return pltpu.make_async_remote_copy(
            src_ref=mixed_out.at[lanes(to, block_rows), :],
            dst_ref=mixed_in.at[:, lanes(my_block, columns)],
            send_sem=back_send.at[hop],
            recv_sem=back_recv.at[hop],
            device_id={"ctx": to},
        )

    def convolve(block):
        def term(step, total):
            later = block * block_rows - step * TILE + TILE
            left = toeplitz[pl.ds(pl.multiple_of(later, TILE), block_rows), :]
            right = kv_seq[lanes(step, TILE), :]
            return total + jnp.dot(left, right, preferred_element_type=jnp.float32)

        start = jnp.zeros((block_rows, columns), jnp.float32)
        total = lax.fori_loop(0, (block + 1) * (block_rows // TILE), term, start)
        here = lanes(block, block_rows)
        mixed_out[here, :] = (total + gain * kv_seq[here, :].astype(jnp.float32)).astype(jnp.bfloat16)

    back_copies = []
    for hop in range(1, blocks):
        convolve(other_block(hop))
        copy = returning(hop)
        copy.start()
        back_copies.append(copy)
    convolve(my_block)
    mixed_in[:, lanes(my_block, columns)] = mixed_out[lanes(my_block, block_rows), :]

    for copy in query_copies:
        copy.wait_recv()

    def gate(hop):
        here = lanes(other_block(-hop), columns)
        product = query_rows[:, here].astype(jnp.float32) * mixed_in[:, here].astype(jnp.float32)
        out_ref[:, here] = product.astype(jnp.bfloat16)

    gate(0)
    for hop in range(1, blocks):
        back_copies[hop - 1].wait_recv()
        gate(hop)
    for copy in kv_copies + query_copies + seq_copies + back_copies:
        copy.wait_send()


def by_products(projected, short_taps, long_filter, skip_gain):
    chans = lax.axis_size("chan")
    blocks = lax.axis_size("ctx")
    my_chan = lax.axis_index("chan")
    my_block = lax.axis_index("ctx")
    own = projected[0]
    rows, _, channels = own.shape
    width = skip_gain.shape[0]
    columns = width // blocks
    per_group = width // long_filter.shape[1]
    length = rows * chans * blocks
    last = own[rows - (TAPS - 1) :]
    pairs = []
    for at in range(blocks * chans - 1):
        source = (at % chans) * blocks + at // chans
        after = at + 1
        pairs.append((source, (after % chans) * blocks + after // chans))
    earlier = lax.ppermute(last, ("chan", "ctx"), pairs)
    queries, product = featurize(earlier, own, short_taps)

    group = my_block * columns // per_group
    lags = lax.all_gather(long_filter.T, "ctx", axis=1, tiled=True)
    lags = lax.dynamic_slice_in_dim(lags, group, 1, 0)
    lags = jnp.pad(jnp.flip(lags, 1), ((0, 0), (0, TILE)))
    gains = lax.dynamic_slice_in_dim(skip_gain, my_block * columns, columns, 0)[None]

    block_rows = rows * chans
    vmem = pl.BlockSpec(memory_space=pltpu.VMEM)
    dma = pltpu.SemaphoreType.DMA
    return pl.pallas_call(
        exchange_kernel,
        out_shape=jax.ShapeDtypeStruct((block_rows, width), jnp.bfloat16),
        in_specs=[vmem] * 4,
        out_specs=vmem,
        scratch_shapes=[
            pltpu.VMEM((block_rows, width), jnp.bfloat16),
            pltpu.VMEM((block_rows, width), jnp.bfloat16),
            pltpu.VMEM((length, columns), jnp.bfloat16),
            pltpu.VMEM((length, columns), jnp.bfloat16),
            pltpu.VMEM((block_rows, width), jnp.bfloat16),
            pltpu.VMEM((length + TILE, TILE), jnp.bfloat16),
            dma((chans,)),
            dma((chans,)),
            dma((chans,)),
            dma((chans,)),
            dma((chans, blocks)),
            dma((chans, blocks)),
            dma((blocks,)),
            dma((blocks,)),
        ],
        compiler_params=pltpu.CompilerParams(
            collective_id=0, has_side_effects=True, vmem_limit_bytes=40 * 1024 * 1024
        ),
    )(queries, product, lags, gains)


def local(projected, short_taps, long_filter, skip_gain):
    chans = lax.axis_size("chan")
    blocks = lax.axis_size("ctx")
    rows = projected.shape[1]
    width = skip_gain.shape[0]
    columns = width // blocks
    per_group = width // long_filter.shape[1]
    fits = columns % 128 == 0 and per_group % columns == 0
    fits = fits and rows % 16 == 0 and rows * chans % TILE == 0
    if fits:
        return by_products(projected, short_taps, long_filter, skip_gain)
    return by_transform(projected, short_taps, long_filter, skip_gain)


def solution(mesh):
    placed = (P("ctx", "chan", None, None), P(), P("ctx", "chan"), P("chan"))
    return jax.shard_map(
        local, mesh=mesh, in_specs=placed, out_specs=P("ctx", "chan"), check_vma=False
    )
```

```python
import functools
import math

import jax
import jax.numpy as jnp
from jax import lax
from jax.experimental import pallas as pl
from jax.experimental.pallas import tpu as pltpu
from jax.sharding import PartitionSpec as P

TAPS = 3


PRECISE = lax.Precision.HIGHEST


def passed_along(value, axis, by):
    count = lax.axis_size(axis)
    pairs = [(i, i + by) for i in range(count) if 0 <= i + by < count]
    return lax.ppermute(value, axis, pairs)


def counting(length):
    return jnp.arange(length, dtype=jnp.int32)


def phases(first, second, length):
    turned = first[:, None] * second[None, :] % length
    angles = turned.astype(jnp.float32) * (2.0 * math.pi / length)
    return (jnp.cos(angles), jnp.sin(angles))


def rotate(real_part, imag_part, cosines, sines, direction):
    return (
        real_part * cosines - direction * imag_part * sines,
        imag_part * cosines + direction * real_part * sines,
    )


def complex_mix(pattern, cosines, sines, real_part, imag_part, direction):
    cos_real = jnp.einsum(pattern, cosines, real_part, precision=PRECISE)
    sin_real = jnp.einsum(pattern, sines, real_part, precision=PRECISE)
    if imag_part is None:
        return (cos_real, direction * sin_real)
    cos_imag = jnp.einsum(pattern, cosines, imag_part, precision=PRECISE)
    sin_imag = jnp.einsum(pattern, sines, imag_part, precision=PRECISE)
    return (cos_real - direction * sin_imag, cos_imag + direction * sin_real)


def leading_factor(length):
    chosen = 1
    for option in range(1, math.isqrt(length) + 1):
        if length % option == 0:
            chosen = option
    return chosen


def local_tables(first, second):
    cos_one, sin_one = phases(counting(first), counting(first), first)
    cos_two, sin_two = phases(counting(second), counting(second), second)
    cos_mid, sin_mid = phases(counting(first), counting(second), first * second)
    return (
        cos_one,
        sin_one,
        cos_two,
        sin_two,
        cos_mid[None, :, :, None],
        sin_mid[None, :, :, None],
    )


def inner_forward(real_part, imag_part):
    leading, length, columns = real_part.shape
    first = leading_factor(length)
    second = length // first
    cos_one, sin_one, cos_two, sin_two, cos_mid, sin_mid = local_tables(first, second)
    real_part = real_part.reshape(leading, first, second, columns)
    if imag_part is not None:
        imag_part = imag_part.reshape(leading, first, second, columns)
    real_part, imag_part = complex_mix(
        "bk,akjx->abjx", cos_one, sin_one, real_part, imag_part, -1.0
    )
    real_part, imag_part = rotate(real_part, imag_part, cos_mid, sin_mid, -1.0)
    return complex_mix("ej,abjx->abex", cos_two, sin_two, real_part, imag_part, -1.0)


def inner_inverse(real_part, imag_part):
    leading, first, second, columns = real_part.shape
    cos_one, sin_one, cos_two, sin_two, cos_mid, sin_mid = local_tables(first, second)
    real_part, imag_part = complex_mix("ej,abjx->abex", cos_two, sin_two, real_part, imag_part, 1.0)
    real_part, imag_part = rotate(real_part, imag_part, cos_mid, sin_mid, 1.0)
    real_part, imag_part = complex_mix("kb,abjx->akjx", cos_one, sin_one, real_part, imag_part, 1.0)
    return (
        real_part.reshape(leading, first * second, columns),
        imag_part.reshape(leading, first * second, columns),
    )


def featurize(earlier, own_rows, filter_taps):
    lag_rows = earlier.shape[0]
    length = own_rows.shape[0]
    extended = jnp.concatenate([earlier, own_rows], axis=0).astype(jnp.float32)
    weights = filter_taps.astype(jnp.float32)
    summed = weights[0] * extended[lag_rows : lag_rows + length]
    for offset in range(1, weights.shape[0]):
        summed = summed + weights[offset] * extended[lag_rows - offset : lag_rows - offset + length]
    queries = lax.optimization_barrier(summed[:, 0].astype(jnp.bfloat16))
    product = (summed[:, 1] * summed[:, 2]).astype(jnp.bfloat16)
    return (queries, product)


def whole_transform(real_part, imag_part):
    zeros = jnp.zeros_like(real_part)
    padded_real = jnp.concatenate([real_part, zeros], axis=0)[None]
    padded_imag = None
    if imag_part is not None:
        padded_imag = jnp.concatenate([imag_part, zeros], axis=0)[None]
    return inner_forward(padded_real, padded_imag)


def local_convolve(signal, filters, gains_here, position, per_group):
    length, columns = signal.shape
    groups_here = filters.shape[1]
    first_channel = position * columns
    pairs = signal.reshape(length, columns // 2, 2)
    real_in = pairs[:, :, 0]
    imag_in = pairs[:, :, 1]
    owners = (first_channel + 2 * counting(columns // 2)) // per_group
    selector = (counting(groups_here)[:, None] == owners[None, :]).astype(jnp.float32)
    filt_real, filt_imag = whole_transform(filters, None)
    filt_real = jnp.einsum("abex,xc->abec", filt_real, selector, precision=PRECISE)
    filt_imag = jnp.einsum("abex,xc->abec", filt_imag, selector, precision=PRECISE)
    sig_real, sig_imag = whole_transform(real_in, imag_in)
    prod_real = sig_real * filt_real - sig_imag * filt_imag
    prod_imag = sig_real * filt_imag + sig_imag * filt_real
    back_real, back_imag = inner_inverse(prod_real, prod_imag)
    inverse_scale = 1.0 / (2 * length)
    conv_real = back_real[0, :length] * inverse_scale
    conv_imag = back_imag[0, :length] * inverse_scale
    convolved = jnp.stack([conv_real, conv_imag], axis=2).reshape(length, columns)
    return convolved + gains_here * signal


def by_transform(projected, short_taps, long_filter, skip_gain):
    devices = lax.axis_size("ctx")
    position = lax.axis_index("ctx")
    channel_slot = lax.axis_index("chan")
    channels = skip_gain.shape[0]
    groups_here = long_filter.shape[1]
    per_group = channels // groups_here
    regrouped = lax.all_to_all(projected, "chan", split_axis=3, concat_axis=1, tiled=True)[0]
    taps_here = lax.dynamic_slice_in_dim(short_taps, channel_slot * channels, channels, 2)
    last_rows = regrouped[regrouped.shape[0] - (TAPS - 1) :]
    earlier = passed_along(last_rows, "ctx", 1)
    queries, product = featurize(earlier, regrouped, taps_here)
    kv_seq = lax.all_to_all(product[None], "ctx", split_axis=2, concat_axis=0, tiled=True)
    block_rows = kv_seq.shape[1]
    columns = kv_seq.shape[2]
    signal = kv_seq.reshape(devices * block_rows, columns).astype(jnp.float32)
    filters = lax.all_gather(long_filter, "ctx", axis=0, tiled=True)
    gains_here = lax.dynamic_slice_in_dim(skip_gain, position * columns, columns, 0)
    mixed = local_convolve(signal, filters, gains_here, position, per_group).astype(jnp.bfloat16)
    mixed = mixed.reshape(devices, block_rows, columns)
    mixed_rows = lax.all_to_all(mixed, "ctx", split_axis=0, concat_axis=2, tiled=True)[0]
    return (queries.astype(jnp.float32) * mixed_rows.astype(jnp.float32)).astype(jnp.bfloat16)


TILE = 256


EDGE = 16


def exchange_kernel(
    per_group,
    own_ref,
    taps_ref,
    lags_ref,
    gain_ref,
    out_ref,
    halo_out,
    halo_in,
    lags_out,
    lags_in,
    lags_line,
    query_out,
    kv_out,
    query_rows,
    kv_rows,
    kv_seq,
    mixed_out,
    mixed_in,
    toeplitz,
    halo_send,
    halo_recv,
    lags_send,
    lags_recv,
    kv_send,
    kv_recv,
    query_send,
    query_recv,
    seq_send,
    seq_recv,
    back_send,
    back_recv,
):
    chans = lax.axis_size("chan")
    blocks = lax.axis_size("ctx")
    my_chan = lax.axis_index("chan")
    my_block = lax.axis_index("ctx")
    rows = own_ref.shape[1]
    width = kv_rows.shape[1]
    length, columns = kv_seq.shape
    block_rows = rows * chans

    def other_chan(step):
        return lax.rem(my_chan + step + chans, chans)

    def other_block(step):
        return lax.rem(my_block + step + blocks, blocks)

    def lanes(index, size):
        return pl.ds(pl.multiple_of(index * size, size), size)

    is_first = my_chan == 0
    is_last = my_chan == chans - 1
    previous = {"chan": other_chan(-1), "ctx": jnp.where(is_first, other_block(-1), my_block)}
    following = {"chan": other_chan(1), "ctx": jnp.where(is_last, other_block(1), my_block)}
    starts = jnp.logical_and(is_first, my_block == 0)

    barrier = pltpu.get_barrier_semaphore()
    for step in range(1, chans):
        pl.semaphore_signal(barrier, inc=1, device_id={"chan": other_chan(step)})
    for step in range(1, blocks):
        pl.semaphore_signal(barrier, inc=1, device_id={"ctx": other_block(step)})
    pl.semaphore_signal(barrier, inc=1, device_id=previous)

    for part in range(3):
        edge = own_ref[part, rows - EDGE :, :].astype(jnp.float32)
        halo_out[2 * part : 2 * part + 2, :] = edge[EDGE - 2 :]
    halo_out[6:8, :] = jnp.zeros((2, halo_out.shape[1]), jnp.float32)
    span = lags_ref.shape[1]
    across = lax.broadcasted_iota(jnp.int32, (span, span), 0)
    down = lax.broadcasted_iota(jnp.int32, (span, span), 1)
    flip = (across + down == span - 1).astype(jnp.bfloat16)
    lags_out[...] = jnp.dot(
        lags_ref[...].astype(jnp.bfloat16), flip, preferred_element_type=jnp.float32
    )
    lags_in[my_block] = lags_out[...]

    piece = 256

    def feature(part, count, here, with_halo):
        value = own_ref[part, 0:count, here].astype(jnp.float32)
        at = lax.broadcasted_iota(jnp.int32, value.shape, 0)
        total = None
        for offset in range(TAPS):
            weight = taps_ref[offset, :, here].astype(jnp.float32)[part : part + 1]
            moved = value
            if offset:
                moved = pltpu.roll(value, offset, 0)
                if with_halo:
                    for k in range(offset):
                        row = 2 * part + 2 + k - offset
                        edge = jnp.where(starts, 0.0, halo_in[row : row + 1, here])
                        moved = jnp.where(at == k, edge, moved)
            total = weight * moved if total is None else total + weight * moved
        return total

    def make_kv(target, at_row, count, chan, first_lane, with_halo):
        @pl.loop(0, width // piece)
        def _(index):
            here = pl.ds(pl.multiple_of(chan * width + index * piece, piece), piece)
            there = pl.ds(pl.multiple_of(first_lane + index * piece, piece), piece)
            product = feature(1, count, here, with_halo) * feature(2, count, here, with_halo)
            target[pl.ds(at_row, count), there] = product.astype(jnp.bfloat16)

    def make_query(target, at_row, chan, first_lane):
        @pl.loop(0, width // piece)
        def _(index):
            here = pl.ds(pl.multiple_of(chan * width + index * piece, piece), piece)
            there = pl.ds(pl.multiple_of(first_lane + index * piece, piece), piece)
            target[pl.ds(at_row, rows), there] = feature(0, rows, here, True).astype(jnp.bfloat16)

    def over_chan(source, target, send, recv, step, first_row, count):
        to = other_chan(step)
        there = pl.multiple_of(my_chan * rows + first_row, EDGE)
        return pltpu.make_async_remote_copy(
            src_ref=source.at[pl.ds(first_row, count), lanes(to, width)],
            dst_ref=target.at[pl.ds(there, count), :],
            send_sem=send,
            recv_sem=recv,
            device_id={"chan": to},
        )

    make_kv(kv_out, 0, rows, other_chan(1), other_chan(1) * width, False)
    pl.semaphore_wait(barrier, chans + blocks - 1)

    halo_copy = pltpu.make_async_remote_copy(
        src_ref=halo_out,
        dst_ref=halo_in,
        send_sem=halo_send,
        recv_sem=halo_recv,
        device_id=following,
    )
    halo_copy.start()

    low_copies = [
        over_chan(kv_out, kv_rows, kv_send.at[0, k], kv_recv.at[0, k], k, EDGE, rows - EDGE)
        for k in range(1, chans)
    ]
    edge_copies = [
        over_chan(kv_out, kv_rows, kv_send.at[1, k], kv_recv.at[1, k], k, 0, EDGE)
        for k in range(1, chans)
    ]
    query_copies = [
        over_chan(query_out, query_rows, query_send.at[k], query_recv.at[k], k, 0, rows)
        for k in range(1, chans)
    ]
    low_copies[0].start()
    for step in range(2, chans):
        to = other_chan(step)
        make_kv(kv_out, 0, rows, to, to * width, False)
        low_copies[step - 1].start()
    lags_copies = []
    for hop in range(1, blocks):
        copy = pltpu.make_async_remote_copy(
            src_ref=lags_out,
            dst_ref=lags_in.at[my_block],
            send_sem=lags_send.at[hop],
            recv_sem=lags_recv.at[hop],
            device_id={"ctx": other_block(hop)},
        )
        copy.start()
        lags_copies.append(copy)
    my_rows = pl.multiple_of(my_chan * rows, rows)

    halo_copy.wait_recv()
    for step in range(1, chans):
        to = other_chan(step)
        make_kv(kv_out, 0, EDGE, to, to * width, True)
        edge_copies[step - 1].start()
    make_kv(kv_rows, my_rows, rows, my_chan, 0, True)

    seq_copies = []

    def forward(step):
        origin = other_chan(-step)
        here = lanes(origin, rows)
        there = lanes(my_block * chans + origin, rows)
        for hop in range(1, blocks):
            to = other_block(hop)
            copy = pltpu.make_async_remote_copy(
                src_ref=kv_rows.at[here, lanes(to, columns)],
                dst_ref=kv_seq.at[there, :],
                send_sem=seq_send.at[step, hop],
                recv_sem=seq_recv.at[step, hop],
                device_id={"ctx": to},
            )
            copy.start()
            seq_copies.append(copy)
        kv_seq[there, :] = kv_rows[here, lanes(my_block, columns)]

    forward(0)
    for step in range(1, chans):
        to = other_chan(step)
        make_query(query_out, 0, to, to * width)
    make_query(query_rows, my_rows, my_chan, 0)

    for copy in lags_copies:
        copy.wait_recv()
    group = my_block * columns // per_group
    for block in range(blocks):
        first = (blocks - 1 - block) * span
        lags_line[:, first : first + span] = lags_in[block, pl.ds(group, 1), :]
    lags_line[:, length:] = jnp.zeros((1, TILE), jnp.float32)

    tiles = length // TILE
    bands = block_rows // TILE
    for tile in range(tiles):
        first = length - TILE - tile * TILE
        window = jnp.broadcast_to(lags_line[:, first : first + 2 * TILE], (TILE, 2 * TILE))
        turned = pltpu.roll(window, TILE + 1, 1, stride=1, stride_axis=0)
        turned = turned[:, :TILE].astype(jnp.bfloat16)
        for band in range(bands):
            column = tiles - bands + band - tile
            if column >= 0:
                toeplitz[
                    band * TILE : (band + 1) * TILE, column * TILE : (column + 1) * TILE
                ] = turned
    for band in range(bands):
        for column in range(tiles - bands + band + 1, tiles):
            toeplitz[
                band * TILE : (band + 1) * TILE, column * TILE : (column + 1) * TILE
            ] = jnp.zeros((TILE, TILE), jnp.bfloat16)

    for step in range(1, chans):
        low_copies[step - 1].wait_recv()
        edge_copies[step - 1].wait_recv()
        forward(step)
        low_copies[step - 1].wait_send()
        query_copies[step - 1].start()
    for copy in seq_copies:
        copy.wait_recv()

    gain = gain_ref[...]

    def returning(hop):
        to = other_block(hop)
        return pltpu.make_async_remote_copy(
            src_ref=mixed_out.at[lanes(to, block_rows), :],
            dst_ref=mixed_in.at[:, lanes(my_block, columns)],
            send_sem=back_send.at[hop],
            recv_sem=back_recv.at[hop],
            device_id={"ctx": to},
        )

    def convolve(block):
        def term(step, total):
            left = toeplitz[:, lanes(blocks - 1 - block + step, block_rows)]
            right = kv_seq[lanes(step, block_rows), :]
            return total + jnp.dot(left, right, preferred_element_type=jnp.float32)

        start = jnp.zeros((block_rows, columns), jnp.float32)
        total = lax.fori_loop(0, block + 1, term, start)
        here = lanes(block, block_rows)
        mixed_out[here, :] = (total + gain * kv_seq[here, :].astype(jnp.float32)).astype(jnp.bfloat16)

    back_copies = []
    for hop in range(1, blocks):
        convolve(other_block(hop))
        copy = returning(hop)
        copy.start()
        back_copies.append(copy)
    convolve(my_block)
    mixed_in[:, lanes(my_block, columns)] = mixed_out[lanes(my_block, block_rows), :]

    for copy in query_copies:
        copy.wait_recv()

    def gate(hop):
        here = lanes(other_block(-hop), columns)
        product = query_rows[:, here].astype(jnp.float32) * mixed_in[:, here].astype(jnp.float32)
        out_ref[:, here] = product.astype(jnp.bfloat16)

    gate(0)
    for hop in range(1, blocks):
        back_copies[hop - 1].wait_recv()
        gate(hop)
    for copy in edge_copies + query_copies + seq_copies + back_copies:
        copy.wait_send()
    for copy in lags_copies + [halo_copy]:
        copy.wait_send()


def by_products(projected, short_taps, long_filter, skip_gain):
    chans = lax.axis_size("chan")
    blocks = lax.axis_size("ctx")
    my_block = lax.axis_index("ctx")
    own = projected[0].transpose(1, 0, 2)
    _, rows, channels = own.shape
    width = skip_gain.shape[0]
    columns = width // blocks
    groups, span = long_filter.shape[1], long_filter.shape[0]
    length = rows * chans * blocks
    gains = lax.dynamic_slice_in_dim(skip_gain, my_block * columns, columns, 0)[None]

    block_rows = rows * chans
    vmem = pl.BlockSpec(memory_space=pltpu.VMEM)
    dma = pltpu.SemaphoreType.DMA
    return pl.pallas_call(
        functools.partial(exchange_kernel, width // groups),
        out_shape=jax.ShapeDtypeStruct((block_rows, width), jnp.bfloat16),
        in_specs=[vmem] * 4,
        out_specs=vmem,
        scratch_shapes=[
            pltpu.VMEM((8, channels), jnp.float32),
            pltpu.VMEM((8, channels), jnp.float32),
            pltpu.VMEM((groups, span), jnp.float32),
            pltpu.VMEM((blocks, groups, span), jnp.float32),
            pltpu.VMEM((1, length + TILE), jnp.float32),
            pltpu.VMEM((rows, channels), jnp.bfloat16),
            pltpu.VMEM((rows, channels), jnp.bfloat16),
            pltpu.VMEM((block_rows, width), jnp.bfloat16),
            pltpu.VMEM((block_rows, width), jnp.bfloat16),
            pltpu.VMEM((length, columns), jnp.bfloat16),
            pltpu.VMEM((length, columns), jnp.bfloat16),
            pltpu.VMEM((block_rows, width), jnp.bfloat16),
            pltpu.VMEM((block_rows, length), jnp.bfloat16),
            dma(()),
            dma(()),
            dma((blocks,)),
            dma((blocks,)),
            dma((2, chans)),
            dma((2, chans)),
            dma((chans,)),
            dma((chans,)),
            dma((chans, blocks)),
            dma((chans, blocks)),
            dma((blocks,)),
            dma((blocks,)),
        ],
        compiler_params=pltpu.CompilerParams(
            collective_id=0, has_side_effects=True, vmem_limit_bytes=48 * 1024 * 1024
        ),
    )(own, short_taps, long_filter.T, gains)


def local(projected, short_taps, long_filter, skip_gain):
    chans = lax.axis_size("chan")
    blocks = lax.axis_size("ctx")
    rows = projected.shape[1]
    width = skip_gain.shape[0]
    columns = width // blocks
    per_group = width // long_filter.shape[1]
    fits = columns % 128 == 0 and per_group % columns == 0
    fits = fits and rows % 32 == 0 and rows * chans % TILE == 0 and width % 256 == 0
    fits = fits and per_group % 128 == 0
    if fits:
        return by_products(projected, short_taps, long_filter, skip_gain)
    return by_transform(projected, short_taps, long_filter, skip_gain)


def solution(mesh):
    placed = (P("ctx", "chan", None, None), P(), P("ctx", "chan"), P("chan"))
    return jax.shard_map(
        local, mesh=mesh, in_specs=placed, out_specs=P("ctx", "chan"), check_vma=False
    )
```

```python
import functools
import math

import jax
import jax.numpy as jnp
from jax import lax
from jax.experimental import pallas as pl
from jax.experimental.pallas import tpu as pltpu
from jax.sharding import PartitionSpec as P

TAPS = 3


PRECISE = lax.Precision.HIGHEST


def passed_along(value, axis, by):
    count = lax.axis_size(axis)
    pairs = [(i, i + by) for i in range(count) if 0 <= i + by < count]
    return lax.ppermute(value, axis, pairs)


def counting(length):
    return jnp.arange(length, dtype=jnp.int32)


def phases(first, second, length):
    turned = first[:, None] * second[None, :] % length
    angles = turned.astype(jnp.float32) * (2.0 * math.pi / length)
    return (jnp.cos(angles), jnp.sin(angles))


def rotate(real_part, imag_part, cosines, sines, direction):
    return (
        real_part * cosines - direction * imag_part * sines,
        imag_part * cosines + direction * real_part * sines,
    )


def complex_mix(pattern, cosines, sines, real_part, imag_part, direction):
    cos_real = jnp.einsum(pattern, cosines, real_part, precision=PRECISE)
    sin_real = jnp.einsum(pattern, sines, real_part, precision=PRECISE)
    if imag_part is None:
        return (cos_real, direction * sin_real)
    cos_imag = jnp.einsum(pattern, cosines, imag_part, precision=PRECISE)
    sin_imag = jnp.einsum(pattern, sines, imag_part, precision=PRECISE)
    return (cos_real - direction * sin_imag, cos_imag + direction * sin_real)


def leading_factor(length):
    chosen = 1
    for option in range(1, math.isqrt(length) + 1):
        if length % option == 0:
            chosen = option
    return chosen


def local_tables(first, second):
    cos_one, sin_one = phases(counting(first), counting(first), first)
    cos_two, sin_two = phases(counting(second), counting(second), second)
    cos_mid, sin_mid = phases(counting(first), counting(second), first * second)
    return (
        cos_one,
        sin_one,
        cos_two,
        sin_two,
        cos_mid[None, :, :, None],
        sin_mid[None, :, :, None],
    )


def inner_forward(real_part, imag_part):
    leading, length, columns = real_part.shape
    first = leading_factor(length)
    second = length // first
    cos_one, sin_one, cos_two, sin_two, cos_mid, sin_mid = local_tables(first, second)
    real_part = real_part.reshape(leading, first, second, columns)
    if imag_part is not None:
        imag_part = imag_part.reshape(leading, first, second, columns)
    real_part, imag_part = complex_mix(
        "bk,akjx->abjx", cos_one, sin_one, real_part, imag_part, -1.0
    )
    real_part, imag_part = rotate(real_part, imag_part, cos_mid, sin_mid, -1.0)
    return complex_mix("ej,abjx->abex", cos_two, sin_two, real_part, imag_part, -1.0)


def inner_inverse(real_part, imag_part):
    leading, first, second, columns = real_part.shape
    cos_one, sin_one, cos_two, sin_two, cos_mid, sin_mid = local_tables(first, second)
    real_part, imag_part = complex_mix("ej,abjx->abex", cos_two, sin_two, real_part, imag_part, 1.0)
    real_part, imag_part = rotate(real_part, imag_part, cos_mid, sin_mid, 1.0)
    real_part, imag_part = complex_mix("kb,abjx->akjx", cos_one, sin_one, real_part, imag_part, 1.0)
    return (
        real_part.reshape(leading, first * second, columns),
        imag_part.reshape(leading, first * second, columns),
    )


def featurize(earlier, own_rows, filter_taps):
    lag_rows = earlier.shape[0]
    length = own_rows.shape[0]
    extended = jnp.concatenate([earlier, own_rows], axis=0).astype(jnp.float32)
    weights = filter_taps.astype(jnp.float32)
    summed = weights[0] * extended[lag_rows : lag_rows + length]
    for offset in range(1, weights.shape[0]):
        summed = summed + weights[offset] * extended[lag_rows - offset : lag_rows - offset + length]
    queries = lax.optimization_barrier(summed[:, 0].astype(jnp.bfloat16))
    product = (summed[:, 1] * summed[:, 2]).astype(jnp.bfloat16)
    return (queries, product)


def whole_transform(real_part, imag_part):
    zeros = jnp.zeros_like(real_part)
    padded_real = jnp.concatenate([real_part, zeros], axis=0)[None]
    padded_imag = None
    if imag_part is not None:
        padded_imag = jnp.concatenate([imag_part, zeros], axis=0)[None]
    return inner_forward(padded_real, padded_imag)


def local_convolve(signal, filters, gains_here, position, per_group):
    length, columns = signal.shape
    groups_here = filters.shape[1]
    first_channel = position * columns
    pairs = signal.reshape(length, columns // 2, 2)
    real_in = pairs[:, :, 0]
    imag_in = pairs[:, :, 1]
    owners = (first_channel + 2 * counting(columns // 2)) // per_group
    selector = (counting(groups_here)[:, None] == owners[None, :]).astype(jnp.float32)
    filt_real, filt_imag = whole_transform(filters, None)
    filt_real = jnp.einsum("abex,xc->abec", filt_real, selector, precision=PRECISE)
    filt_imag = jnp.einsum("abex,xc->abec", filt_imag, selector, precision=PRECISE)
    sig_real, sig_imag = whole_transform(real_in, imag_in)
    prod_real = sig_real * filt_real - sig_imag * filt_imag
    prod_imag = sig_real * filt_imag + sig_imag * filt_real
    back_real, back_imag = inner_inverse(prod_real, prod_imag)
    inverse_scale = 1.0 / (2 * length)
    conv_real = back_real[0, :length] * inverse_scale
    conv_imag = back_imag[0, :length] * inverse_scale
    convolved = jnp.stack([conv_real, conv_imag], axis=2).reshape(length, columns)
    return convolved + gains_here * signal


def by_transform(projected, short_taps, long_filter, skip_gain):
    devices = lax.axis_size("ctx")
    position = lax.axis_index("ctx")
    channel_slot = lax.axis_index("chan")
    channels = skip_gain.shape[0]
    groups_here = long_filter.shape[1]
    per_group = channels // groups_here
    regrouped = lax.all_to_all(projected, "chan", split_axis=3, concat_axis=1, tiled=True)[0]
    taps_here = lax.dynamic_slice_in_dim(short_taps, channel_slot * channels, channels, 2)
    last_rows = regrouped[regrouped.shape[0] - (TAPS - 1) :]
    earlier = passed_along(last_rows, "ctx", 1)
    queries, product = featurize(earlier, regrouped, taps_here)
    kv_seq = lax.all_to_all(product[None], "ctx", split_axis=2, concat_axis=0, tiled=True)
    block_rows = kv_seq.shape[1]
    columns = kv_seq.shape[2]
    signal = kv_seq.reshape(devices * block_rows, columns).astype(jnp.float32)
    filters = lax.all_gather(long_filter, "ctx", axis=0, tiled=True)
    gains_here = lax.dynamic_slice_in_dim(skip_gain, position * columns, columns, 0)
    mixed = local_convolve(signal, filters, gains_here, position, per_group).astype(jnp.bfloat16)
    mixed = mixed.reshape(devices, block_rows, columns)
    mixed_rows = lax.all_to_all(mixed, "ctx", split_axis=0, concat_axis=2, tiled=True)[0]
    return (queries.astype(jnp.float32) * mixed_rows.astype(jnp.float32)).astype(jnp.bfloat16)


TILE = 256
PIECES = 4
AHEAD = 2


EDGE = 16


def exchange_kernel(
    per_group,
    own_ref,
    taps_ref,
    lags_ref,
    gain_ref,
    out_ref,
    halo_out,
    halo_in,
    lags_out,
    lags_in,
    lags_line,
    query_out,
    kv_out,
    query_rows,
    kv_rows,
    kv_seq,
    mixed_out,
    mixed_in,
    toeplitz,
    halo_send,
    halo_recv,
    lags_send,
    lags_recv,
    kv_send,
    kv_recv,
    query_send,
    query_recv,
    seq_send,
    seq_recv,
    back_send,
    back_recv,
):
    chans = lax.axis_size("chan")
    blocks = lax.axis_size("ctx")
    my_chan = lax.axis_index("chan")
    my_block = lax.axis_index("ctx")
    rows = own_ref.shape[1]
    width = kv_rows.shape[1]
    length, columns = kv_seq.shape
    block_rows = rows * chans

    def other_chan(step):
        return lax.rem(my_chan + step + chans, chans)

    def other_block(step):
        return lax.rem(my_block + step + blocks, blocks)

    def lanes(index, size):
        return pl.ds(pl.multiple_of(index * size, size), size)

    is_first = my_chan == 0
    is_last = my_chan == chans - 1
    previous = {"chan": other_chan(-1), "ctx": jnp.where(is_first, other_block(-1), my_block)}
    following = {"chan": other_chan(1), "ctx": jnp.where(is_last, other_block(1), my_block)}
    starts = jnp.logical_and(is_first, my_block == 0)

    barrier = pltpu.get_barrier_semaphore()
    for step in range(1, chans):
        pl.semaphore_signal(barrier, inc=1, device_id={"chan": other_chan(step)})
    for step in range(1, blocks):
        pl.semaphore_signal(barrier, inc=1, device_id={"ctx": other_block(step)})
    pl.semaphore_signal(barrier, inc=1, device_id=previous)

    for part in range(3):
        edge = own_ref[part, rows - EDGE :, :].astype(jnp.float32)
        halo_out[2 * part : 2 * part + 2, :] = edge[EDGE - 2 :]
    halo_out[6:8, :] = jnp.zeros((2, halo_out.shape[1]), jnp.float32)
    span = lags_ref.shape[1]
    across = lax.broadcasted_iota(jnp.int32, (span, span), 0)
    down = lax.broadcasted_iota(jnp.int32, (span, span), 1)
    flip = (across + down == span - 1).astype(jnp.bfloat16)
    lags_out[...] = jnp.dot(
        lags_ref[...].astype(jnp.bfloat16), flip, preferred_element_type=jnp.float32
    )
    lags_in[my_block] = lags_out[...]

    piece = 256

    def feature(part, count, here, with_halo):
        value = own_ref[part, 0:count, here].astype(jnp.float32)
        at = lax.broadcasted_iota(jnp.int32, value.shape, 0)
        total = None
        for offset in range(TAPS):
            weight = taps_ref[offset, :, here].astype(jnp.float32)[part : part + 1]
            moved = value
            if offset:
                moved = pltpu.roll(value, offset, 0)
                if with_halo:
                    for k in range(offset):
                        row = 2 * part + 2 + k - offset
                        edge = jnp.where(starts, 0.0, halo_in[row : row + 1, here])
                        moved = jnp.where(at == k, edge, moved)
            total = weight * moved if total is None else total + weight * moved
        return total

    def make_kv(target, at_row, count, chan, first_lane, with_halo):
        @pl.loop(0, width // piece)
        def _(index):
            here = pl.ds(pl.multiple_of(chan * width + index * piece, piece), piece)
            there = pl.ds(pl.multiple_of(first_lane + index * piece, piece), piece)
            product = feature(1, count, here, with_halo) * feature(2, count, here, with_halo)
            target[pl.ds(at_row, count), there] = product.astype(jnp.bfloat16)

    def make_query(target, at_row, chan, first_lane):
        @pl.loop(0, width // piece)
        def _(index):
            here = pl.ds(pl.multiple_of(chan * width + index * piece, piece), piece)
            there = pl.ds(pl.multiple_of(first_lane + index * piece, piece), piece)
            target[pl.ds(at_row, rows), there] = feature(0, rows, here, True).astype(jnp.bfloat16)

    def over_chan(source, target, send, recv, step, first_row, count):
        to = other_chan(step)
        there = pl.multiple_of(my_chan * rows + first_row, EDGE)
        return pltpu.make_async_remote_copy(
            src_ref=source.at[pl.ds(first_row, count), lanes(to, width)],
            dst_ref=target.at[pl.ds(there, count), :],
            send_sem=send,
            recv_sem=recv,
            device_id={"chan": to},
        )

    make_kv(kv_out, 0, rows, other_chan(1), other_chan(1) * width, False)
    pl.semaphore_wait(barrier, chans + blocks - 1)

    halo_copy = pltpu.make_async_remote_copy(
        src_ref=halo_out,
        dst_ref=halo_in,
        send_sem=halo_send,
        recv_sem=halo_recv,
        device_id=following,
    )
    halo_copy.start()

    low_copies = [
        over_chan(kv_out, kv_rows, kv_send.at[0, k], kv_recv.at[0, k], k, EDGE, rows - EDGE)
        for k in range(1, chans)
    ]
    edge_copies = [
        over_chan(kv_out, kv_rows, kv_send.at[1, k], kv_recv.at[1, k], k, 0, EDGE)
        for k in range(1, chans)
    ]
    slab = width // PIECES

    def query_piece(index, step):
        to = other_chan(step)
        lane = pl.multiple_of(to * width + index * slab, slab)
        return pltpu.make_async_remote_copy(
            src_ref=query_out.at[:, pl.ds(lane, slab)],
            dst_ref=query_rows.at[lanes(my_chan, rows), index * slab : (index + 1) * slab],
            send_sem=query_send.at[index, step],
            recv_sem=query_recv.at[index, step],
            device_id={"chan": to},
        )

    query_copies = [[query_piece(i, k) for k in range(1, chans)] for i in range(PIECES)]
    waiting = list(query_copies)

    def send_queries(count):
        for _ in range(min(count, len(waiting))):
            for copy in waiting.pop(0):
                copy.start()

    low_copies[0].start()
    for step in range(2, chans):
        to = other_chan(step)
        make_kv(kv_out, 0, rows, to, to * width, False)
        low_copies[step - 1].start()
    lags_copies = []
    for hop in range(1, blocks):
        copy = pltpu.make_async_remote_copy(
            src_ref=lags_out,
            dst_ref=lags_in.at[my_block],
            send_sem=lags_send.at[hop],
            recv_sem=lags_recv.at[hop],
            device_id={"ctx": other_block(hop)},
        )
        copy.start()
        lags_copies.append(copy)
    my_rows = pl.multiple_of(my_chan * rows, rows)

    halo_copy.wait_recv()
    for step in range(1, chans):
        to = other_chan(step)
        make_kv(kv_out, 0, EDGE, to, to * width, True)
        edge_copies[step - 1].start()
    make_kv(kv_rows, my_rows, rows, my_chan, 0, True)

    seq_copies = []

    def forward(step):
        origin = other_chan(-step)
        here = lanes(origin, rows)
        there = lanes(my_block * chans + origin, rows)
        for hop in range(1, blocks):
            to = other_block(hop)
            copy = pltpu.make_async_remote_copy(
                src_ref=kv_rows.at[here, lanes(to, columns)],
                dst_ref=kv_seq.at[there, :],
                send_sem=seq_send.at[step, hop],
                recv_sem=seq_recv.at[step, hop],
                device_id={"ctx": to},
            )
            copy.start()
            seq_copies.append(copy)
        kv_seq[there, :] = kv_rows[here, lanes(my_block, columns)]

    forward(0)
    for step in range(1, chans):
        to = other_chan(step)
        make_query(query_out, 0, to, to * width)
    make_query(query_rows, my_rows, my_chan, 0)

    for copy in lags_copies:
        copy.wait_recv()
    group = my_block * columns // per_group
    for block in range(blocks):
        first = (blocks - 1 - block) * span
        lags_line[:, first : first + span] = lags_in[block, pl.ds(group, 1), :]
    lags_line[:, length:] = jnp.zeros((1, TILE), jnp.float32)

    tiles = length // TILE
    bands = block_rows // TILE
    for tile in range(tiles):
        first = length - TILE - tile * TILE
        window = jnp.broadcast_to(lags_line[:, first : first + 2 * TILE], (TILE, 2 * TILE))
        turned = pltpu.roll(window, TILE + 1, 1, stride=1, stride_axis=0)
        turned = turned[:, :TILE].astype(jnp.bfloat16)
        for band in range(bands):
            column = tiles - bands + band - tile
            if column >= 0:
                toeplitz[
                    band * TILE : (band + 1) * TILE, column * TILE : (column + 1) * TILE
                ] = turned
    for band in range(bands):
        for column in range(tiles - bands + band + 1, tiles):
            toeplitz[
                band * TILE : (band + 1) * TILE, column * TILE : (column + 1) * TILE
            ] = jnp.zeros((TILE, TILE), jnp.bfloat16)

    for step in range(1, chans):
        low_copies[step - 1].wait_recv()
        edge_copies[step - 1].wait_recv()
        forward(step)
        low_copies[step - 1].wait_send()
    send_queries(AHEAD)
    for copy in seq_copies:
        copy.wait_recv()

    gain = gain_ref[...]

    def returning(hop):
        to = other_block(hop)
        return pltpu.make_async_remote_copy(
            src_ref=mixed_out.at[lanes(to, block_rows), :],
            dst_ref=mixed_in.at[my_block],
            send_sem=back_send.at[hop],
            recv_sem=back_recv.at[hop],
            device_id={"ctx": to},
        )

    def convolve(block):
        def term(step, total):
            left = toeplitz[:, lanes(blocks - 1 - block + step, block_rows)]
            right = kv_seq[lanes(step, block_rows), :]
            return total + jnp.dot(left, right, preferred_element_type=jnp.float32)

        start = jnp.zeros((block_rows, columns), jnp.float32)
        total = lax.fori_loop(0, block + 1, term, start)
        here = lanes(block, block_rows)
        mixed_out[here, :] = (total + gain * kv_seq[here, :].astype(jnp.float32)).astype(jnp.bfloat16)

    back_copies = []
    for hop in range(1, blocks):
        convolve(other_block(hop))
        copy = returning(hop)
        copy.start()
        back_copies.append(copy)
        send_queries(1)
    send_queries(PIECES)
    convolve(my_block)
    mixed_in[my_block] = mixed_out[lanes(my_block, block_rows), :]

    query_copies = [copy for each in query_copies for copy in each]
    for copy in query_copies:
        copy.wait_recv()

    def gate(hop):
        here = lanes(other_block(-hop), columns)
        product = query_rows[:, here].astype(jnp.float32) * mixed_in[other_block(-hop)].astype(jnp.float32)
        out_ref[:, here] = product.astype(jnp.bfloat16)

    gate(0)
    for hop in range(1, blocks):
        back_copies[hop - 1].wait_recv()
        gate(hop)
    for copy in edge_copies + query_copies + seq_copies + back_copies:
        copy.wait_send()
    for copy in lags_copies + [halo_copy]:
        copy.wait_send()


def by_products(projected, short_taps, long_filter, skip_gain):
    chans = lax.axis_size("chan")
    blocks = lax.axis_size("ctx")
    my_block = lax.axis_index("ctx")
    own = projected[0].transpose(1, 0, 2)
    _, rows, channels = own.shape
    width = skip_gain.shape[0]
    columns = width // blocks
    groups, span = long_filter.shape[1], long_filter.shape[0]
    length = rows * chans * blocks
    gains = lax.dynamic_slice_in_dim(skip_gain, my_block * columns, columns, 0)[None]

    block_rows = rows * chans
    vmem = pl.BlockSpec(memory_space=pltpu.VMEM)
    dma = pltpu.SemaphoreType.DMA
    return pl.pallas_call(
        functools.partial(exchange_kernel, width // groups),
        out_shape=jax.ShapeDtypeStruct((block_rows, width), jnp.bfloat16),
        in_specs=[vmem] * 4,
        out_specs=vmem,
        scratch_shapes=[
            pltpu.VMEM((8, channels), jnp.float32),
            pltpu.VMEM((8, channels), jnp.float32),
            pltpu.VMEM((groups, span), jnp.float32),
            pltpu.VMEM((blocks, groups, span), jnp.float32),
            pltpu.VMEM((1, length + TILE), jnp.float32),
            pltpu.VMEM((rows, channels), jnp.bfloat16),
            pltpu.VMEM((rows, channels), jnp.bfloat16),
            pltpu.VMEM((block_rows, width), jnp.bfloat16),
            pltpu.VMEM((block_rows, width), jnp.bfloat16),
            pltpu.VMEM((length, columns), jnp.bfloat16),
            pltpu.VMEM((length, columns), jnp.bfloat16),
            pltpu.VMEM((blocks, block_rows, columns), jnp.bfloat16),
            pltpu.VMEM((block_rows, length), jnp.bfloat16),
            dma(()),
            dma(()),
            dma((blocks,)),
            dma((blocks,)),
            dma((2, chans)),
            dma((2, chans)),
            dma((PIECES, chans)),
            dma((PIECES, chans)),
            dma((chans, blocks)),
            dma((chans, blocks)),
            dma((blocks,)),
            dma((blocks,)),
        ],
        compiler_params=pltpu.CompilerParams(
            collective_id=0, has_side_effects=True, vmem_limit_bytes=48 * 1024 * 1024
        ),
    )(own, short_taps, long_filter.T, gains)


def local(projected, short_taps, long_filter, skip_gain):
    chans = lax.axis_size("chan")
    blocks = lax.axis_size("ctx")
    rows = projected.shape[1]
    width = skip_gain.shape[0]
    columns = width // blocks
    per_group = width // long_filter.shape[1]
    fits = columns % 128 == 0 and per_group % columns == 0
    fits = fits and rows % 32 == 0 and rows * chans % TILE == 0 and width % 256 == 0
    fits = fits and per_group % 128 == 0
    if fits:
        return by_products(projected, short_taps, long_filter, skip_gain)
    return by_transform(projected, short_taps, long_filter, skip_gain)


def solution(mesh):
    placed = (P("ctx", "chan", None, None), P(), P("ctx", "chan"), P("chan"))
    return jax.shard_map(
        local, mesh=mesh, in_specs=placed, out_specs=P("ctx", "chan"), check_vma=False
    )
```

```python
import functools
import math

import jax
import jax.numpy as jnp
from jax import lax
from jax.experimental import pallas as pl
from jax.experimental.pallas import tpu as pltpu
from jax.sharding import PartitionSpec as P

TAPS = 3


PRECISE = lax.Precision.HIGHEST


def passed_along(value, axis, by):
    count = lax.axis_size(axis)
    pairs = [(i, i + by) for i in range(count) if 0 <= i + by < count]
    return lax.ppermute(value, axis, pairs)


def counting(length):
    return jnp.arange(length, dtype=jnp.int32)


def phases(first, second, length):
    turned = first[:, None] * second[None, :] % length
    angles = turned.astype(jnp.float32) * (2.0 * math.pi / length)
    return (jnp.cos(angles), jnp.sin(angles))


def rotate(real_part, imag_part, cosines, sines, direction):
    return (
        real_part * cosines - direction * imag_part * sines,
        imag_part * cosines + direction * real_part * sines,
    )


def complex_mix(pattern, cosines, sines, real_part, imag_part, direction):
    cos_real = jnp.einsum(pattern, cosines, real_part, precision=PRECISE)
    sin_real = jnp.einsum(pattern, sines, real_part, precision=PRECISE)
    if imag_part is None:
        return (cos_real, direction * sin_real)
    cos_imag = jnp.einsum(pattern, cosines, imag_part, precision=PRECISE)
    sin_imag = jnp.einsum(pattern, sines, imag_part, precision=PRECISE)
    return (cos_real - direction * sin_imag, cos_imag + direction * sin_real)


def leading_factor(length):
    chosen = 1
    for option in range(1, math.isqrt(length) + 1):
        if length % option == 0:
            chosen = option
    return chosen


def local_tables(first, second):
    cos_one, sin_one = phases(counting(first), counting(first), first)
    cos_two, sin_two = phases(counting(second), counting(second), second)
    cos_mid, sin_mid = phases(counting(first), counting(second), first * second)
    return (
        cos_one,
        sin_one,
        cos_two,
        sin_two,
        cos_mid[None, :, :, None],
        sin_mid[None, :, :, None],
    )


def inner_forward(real_part, imag_part):
    leading, length, columns = real_part.shape
    first = leading_factor(length)
    second = length // first
    cos_one, sin_one, cos_two, sin_two, cos_mid, sin_mid = local_tables(first, second)
    real_part = real_part.reshape(leading, first, second, columns)
    if imag_part is not None:
        imag_part = imag_part.reshape(leading, first, second, columns)
    real_part, imag_part = complex_mix(
        "bk,akjx->abjx", cos_one, sin_one, real_part, imag_part, -1.0
    )
    real_part, imag_part = rotate(real_part, imag_part, cos_mid, sin_mid, -1.0)
    return complex_mix("ej,abjx->abex", cos_two, sin_two, real_part, imag_part, -1.0)


def inner_inverse(real_part, imag_part):
    leading, first, second, columns = real_part.shape
    cos_one, sin_one, cos_two, sin_two, cos_mid, sin_mid = local_tables(first, second)
    real_part, imag_part = complex_mix("ej,abjx->abex", cos_two, sin_two, real_part, imag_part, 1.0)
    real_part, imag_part = rotate(real_part, imag_part, cos_mid, sin_mid, 1.0)
    real_part, imag_part = complex_mix("kb,abjx->akjx", cos_one, sin_one, real_part, imag_part, 1.0)
    return (
        real_part.reshape(leading, first * second, columns),
        imag_part.reshape(leading, first * second, columns),
    )


def featurize(earlier, own_rows, filter_taps):
    lag_rows = earlier.shape[0]
    length = own_rows.shape[0]
    extended = jnp.concatenate([earlier, own_rows], axis=0).astype(jnp.float32)
    weights = filter_taps.astype(jnp.float32)
    summed = weights[0] * extended[lag_rows : lag_rows + length]
    for offset in range(1, weights.shape[0]):
        summed = summed + weights[offset] * extended[lag_rows - offset : lag_rows - offset + length]
    queries = lax.optimization_barrier(summed[:, 0].astype(jnp.bfloat16))
    product = (summed[:, 1] * summed[:, 2]).astype(jnp.bfloat16)
    return (queries, product)


def whole_transform(real_part, imag_part):
    zeros = jnp.zeros_like(real_part)
    padded_real = jnp.concatenate([real_part, zeros], axis=0)[None]
    padded_imag = None
    if imag_part is not None:
        padded_imag = jnp.concatenate([imag_part, zeros], axis=0)[None]
    return inner_forward(padded_real, padded_imag)


def local_convolve(signal, filters, gains_here, position, per_group):
    length, columns = signal.shape
    groups_here = filters.shape[1]
    first_channel = position * columns
    pairs = signal.reshape(length, columns // 2, 2)
    real_in = pairs[:, :, 0]
    imag_in = pairs[:, :, 1]
    owners = (first_channel + 2 * counting(columns // 2)) // per_group
    selector = (counting(groups_here)[:, None] == owners[None, :]).astype(jnp.float32)
    filt_real, filt_imag = whole_transform(filters, None)
    filt_real = jnp.einsum("abex,xc->abec", filt_real, selector, precision=PRECISE)
    filt_imag = jnp.einsum("abex,xc->abec", filt_imag, selector, precision=PRECISE)
    sig_real, sig_imag = whole_transform(real_in, imag_in)
    prod_real = sig_real * filt_real - sig_imag * filt_imag
    prod_imag = sig_real * filt_imag + sig_imag * filt_real
    back_real, back_imag = inner_inverse(prod_real, prod_imag)
    inverse_scale = 1.0 / (2 * length)
    conv_real = back_real[0, :length] * inverse_scale
    conv_imag = back_imag[0, :length] * inverse_scale
    convolved = jnp.stack([conv_real, conv_imag], axis=2).reshape(length, columns)
    return convolved + gains_here * signal


def by_transform(projected, short_taps, long_filter, skip_gain):
    devices = lax.axis_size("ctx")
    position = lax.axis_index("ctx")
    channel_slot = lax.axis_index("chan")
    channels = skip_gain.shape[0]
    groups_here = long_filter.shape[1]
    per_group = channels // groups_here
    regrouped = lax.all_to_all(projected, "chan", split_axis=3, concat_axis=1, tiled=True)[0]
    taps_here = lax.dynamic_slice_in_dim(short_taps, channel_slot * channels, channels, 2)
    last_rows = regrouped[regrouped.shape[0] - (TAPS - 1) :]
    earlier = passed_along(last_rows, "ctx", 1)
    queries, product = featurize(earlier, regrouped, taps_here)
    kv_seq = lax.all_to_all(product[None], "ctx", split_axis=2, concat_axis=0, tiled=True)
    block_rows = kv_seq.shape[1]
    columns = kv_seq.shape[2]
    signal = kv_seq.reshape(devices * block_rows, columns).astype(jnp.float32)
    filters = lax.all_gather(long_filter, "ctx", axis=0, tiled=True)
    gains_here = lax.dynamic_slice_in_dim(skip_gain, position * columns, columns, 0)
    mixed = local_convolve(signal, filters, gains_here, position, per_group).astype(jnp.bfloat16)
    mixed = mixed.reshape(devices, block_rows, columns)
    mixed_rows = lax.all_to_all(mixed, "ctx", split_axis=0, concat_axis=2, tiled=True)[0]
    return (queries.astype(jnp.float32) * mixed_rows.astype(jnp.float32)).astype(jnp.bfloat16)


TILE = 256
PIECES = 4
AHEAD = 2
EARLY = 1


EDGE = 16


def exchange_kernel(
    per_group,
    own_ref,
    taps_ref,
    lags_ref,
    gain_ref,
    out_ref,
    halo_line,
    halo_out,
    halo_in,
    lags_out,
    lags_in,
    lags_line,
    query_out,
    kv_out,
    query_rows,
    kv_rows,
    kv_seq,
    mixed_out,
    mixed_in,
    toeplitz,
    halo_send,
    halo_recv,
    lags_send,
    lags_recv,
    kv_send,
    kv_recv,
    query_send,
    query_recv,
    seq_send,
    seq_recv,
    back_send,
    back_recv,
):
    chans = lax.axis_size("chan")
    blocks = lax.axis_size("ctx")
    my_chan = lax.axis_index("chan")
    my_block = lax.axis_index("ctx")
    rows = own_ref.shape[1]
    width = kv_rows.shape[1]
    length, columns = kv_seq.shape
    block_rows = rows * chans

    def other_chan(step):
        return lax.rem(my_chan + step + chans, chans)

    def other_block(step):
        return lax.rem(my_block + step + blocks, blocks)

    def lanes(index, size):
        return pl.ds(pl.multiple_of(index * size, size), size)

    is_first = my_chan == 0
    is_last = my_chan == chans - 1
    previous = {"chan": other_chan(-1), "ctx": jnp.where(is_first, other_block(-1), my_block)}
    following = {"chan": other_chan(1), "ctx": jnp.where(is_last, other_block(1), my_block)}
    starts = jnp.logical_and(is_first, my_block == 0)

    barrier = pltpu.get_barrier_semaphore()
    for step in range(1, chans):
        pl.semaphore_signal(barrier, inc=1, device_id={"chan": other_chan(step)})
    for step in range(1, blocks):
        pl.semaphore_signal(barrier, inc=1, device_id={"ctx": other_block(step)})
    pl.semaphore_signal(barrier, inc=1, device_id=previous)

    for part in range(3):
        edge = own_ref[part, rows - EDGE :, :].astype(jnp.float32)
        halo_line[2 * part : 2 * part + 2, :] = edge[EDGE - 2 :]
    halo_line[6:8, :] = jnp.zeros((2, halo_line.shape[1]), jnp.float32)
    half = halo_out.shape[1]
    halves = [halo_line[:, :half], halo_line[:, half:]]
    halo_out[...] = jnp.concatenate(halves, axis=0).astype(jnp.bfloat16)
    span = lags_ref.shape[1]
    across = lax.broadcasted_iota(jnp.int32, (span, span), 0)
    down = lax.broadcasted_iota(jnp.int32, (span, span), 1)
    flip = (across + down == span - 1).astype(jnp.bfloat16)
    lags_out[...] = jnp.dot(
        lags_ref[...].astype(jnp.bfloat16), flip, preferred_element_type=jnp.float32
    )
    lags_in[my_block] = lags_out[...]

    piece = 256

    def feature(part, count, here, with_halo):
        value = own_ref[part, 0:count, here].astype(jnp.float32)
        at = lax.broadcasted_iota(jnp.int32, value.shape, 0)
        total = None
        for offset in range(TAPS):
            weight = taps_ref[offset, :, here].astype(jnp.float32)[part : part + 1]
            moved = value
            if offset:
                moved = pltpu.roll(value, offset, 0)
                if with_halo:
                    for k in range(offset):
                        row = 2 * part + 2 + k - offset
                        edge = jnp.where(starts, 0.0, halo_line[row : row + 1, here])
                        moved = jnp.where(at == k, edge, moved)
            total = weight * moved if total is None else total + weight * moved
        return total

    def make_kv(target, at_row, count, chan, first_lane, with_halo):
        @pl.loop(0, width // piece)
        def _(index):
            here = pl.ds(pl.multiple_of(chan * width + index * piece, piece), piece)
            there = pl.ds(pl.multiple_of(first_lane + index * piece, piece), piece)
            product = feature(1, count, here, with_halo) * feature(2, count, here, with_halo)
            target[pl.ds(at_row, count), there] = product.astype(jnp.bfloat16)

    def make_query(target, at_row, chan, first_lane):
        @pl.loop(0, width // piece)
        def _(index):
            here = pl.ds(pl.multiple_of(chan * width + index * piece, piece), piece)
            there = pl.ds(pl.multiple_of(first_lane + index * piece, piece), piece)
            target[pl.ds(at_row, rows), there] = feature(0, rows, here, True).astype(jnp.bfloat16)

    def over_chan(source, target, send, recv, step, first_row, count):
        to = other_chan(step)
        there = pl.multiple_of(my_chan * rows + first_row, EDGE)
        return pltpu.make_async_remote_copy(
            src_ref=source.at[pl.ds(first_row, count), lanes(to, width)],
            dst_ref=target.at[pl.ds(there, count), :],
            send_sem=send,
            recv_sem=recv,
            device_id={"chan": to},
        )

    make_kv(kv_out, 0, rows, other_chan(1), other_chan(1) * width, False)
    pl.semaphore_wait(barrier, chans + blocks - 1)

    halo_copy = pltpu.make_async_remote_copy(
        src_ref=halo_out,
        dst_ref=halo_in,
        send_sem=halo_send,
        recv_sem=halo_recv,
        device_id=following,
    )
    halo_copy.start()

    low_copies = [
        over_chan(kv_out, kv_rows, kv_send.at[0, k], kv_recv.at[0, k], k, EDGE, rows - EDGE)
        for k in range(1, chans)
    ]
    edge_copies = [
        over_chan(kv_out, kv_rows, kv_send.at[1, k], kv_recv.at[1, k], k, 0, EDGE)
        for k in range(1, chans)
    ]
    slab = width // PIECES

    def query_piece(index, step):
        to = other_chan(step)
        lane = pl.multiple_of(to * width + index * slab, slab)
        return pltpu.make_async_remote_copy(
            src_ref=query_out.at[:, pl.ds(lane, slab)],
            dst_ref=query_rows.at[lanes(my_chan, rows), index * slab : (index + 1) * slab],
            send_sem=query_send.at[index, step],
            recv_sem=query_recv.at[index, step],
            device_id={"chan": to},
        )

    query_copies = [[query_piece(i, k) for k in range(1, chans)] for i in range(PIECES)]
    waiting = list(query_copies)

    def send_queries(count):
        for _ in range(min(count, len(waiting))):
            for copy in waiting.pop(0):
                copy.start()

    low_copies[0].start()
    for step in range(2, chans):
        to = other_chan(step)
        make_kv(kv_out, 0, rows, to, to * width, False)
        low_copies[step - 1].start()
    lags_copies = []
    for hop in range(1, blocks):
        copy = pltpu.make_async_remote_copy(
            src_ref=lags_out,
            dst_ref=lags_in.at[my_block],
            send_sem=lags_send.at[hop],
            recv_sem=lags_recv.at[hop],
            device_id={"ctx": other_block(hop)},
        )
        copy.start()
        lags_copies.append(copy)
    my_rows = pl.multiple_of(my_chan * rows, rows)

    halo_copy.wait_recv()
    arrived = halo_in[...].astype(jnp.float32)
    halo_line[:, :half] = arrived[:8]
    halo_line[:, half:] = arrived[8:]
    for step in range(1, chans):
        to = other_chan(step)
        make_kv(kv_out, 0, EDGE, to, to * width, True)
        edge_copies[step - 1].start()
    make_kv(kv_rows, my_rows, rows, my_chan, 0, True)

    seq_copies = []

    def forward(step):
        origin = other_chan(-step)
        here = lanes(origin, rows)
        there = lanes(my_block * chans + origin, rows)
        for hop in range(1, blocks):
            to = other_block(hop)
            copy = pltpu.make_async_remote_copy(
                src_ref=kv_rows.at[here, lanes(to, columns)],
                dst_ref=kv_seq.at[there, :],
                send_sem=seq_send.at[step, hop],
                recv_sem=seq_recv.at[step, hop],
                device_id={"ctx": to},
            )
            copy.start()
            seq_copies.append(copy)
        kv_seq[there, :] = kv_rows[here, lanes(my_block, columns)]

    forward(0)
    for step in range(1, chans):
        to = other_chan(step)
        make_query(query_out, 0, to, to * width)
    make_query(query_rows, my_rows, my_chan, 0)

    for copy in lags_copies:
        copy.wait_recv()
    group = my_block * columns // per_group
    for block in range(blocks):
        first = (blocks - 1 - block) * span
        lags_line[:, first : first + span] = lags_in[block, pl.ds(group, 1), :]
    lags_line[:, length:] = jnp.zeros((1, TILE), jnp.float32)

    tiles = length // TILE
    bands = block_rows // TILE
    for tile in range(tiles):
        first = length - TILE - tile * TILE
        window = jnp.broadcast_to(lags_line[:, first : first + 2 * TILE], (TILE, 2 * TILE))
        turned = pltpu.roll(window, TILE + 1, 1, stride=1, stride_axis=0)
        turned = turned[:, :TILE].astype(jnp.bfloat16)
        for band in range(bands):
            column = tiles - bands + band - tile
            if column >= 0:
                toeplitz[
                    band * TILE : (band + 1) * TILE, column * TILE : (column + 1) * TILE
                ] = turned
    for band in range(bands):
        for column in range(tiles - bands + band + 1, tiles):
            toeplitz[
                band * TILE : (band + 1) * TILE, column * TILE : (column + 1) * TILE
            ] = jnp.zeros((TILE, TILE), jnp.bfloat16)

    for step in range(1, chans):
        if step == chans - 1:
            send_queries(EARLY)
        low_copies[step - 1].wait_recv()
        edge_copies[step - 1].wait_recv()
        forward(step)
        low_copies[step - 1].wait_send()
    send_queries(AHEAD - EARLY)
    for copy in seq_copies:
        copy.wait_recv()

    gain = gain_ref[...]

    def returning(hop):
        to = other_block(hop)
        return pltpu.make_async_remote_copy(
            src_ref=mixed_out.at[lanes(to, block_rows), :],
            dst_ref=mixed_in.at[my_block],
            send_sem=back_send.at[hop],
            recv_sem=back_recv.at[hop],
            device_id={"ctx": to},
        )

    def convolve(block):
        def term(step, total):
            left = toeplitz[:, lanes(blocks - 1 - block + step, block_rows)]
            right = kv_seq[lanes(step, block_rows), :]
            return total + jnp.dot(left, right, preferred_element_type=jnp.float32)

        start = jnp.zeros((block_rows, columns), jnp.float32)
        total = lax.fori_loop(0, block + 1, term, start)
        here = lanes(block, block_rows)
        mixed_out[here, :] = (total + gain * kv_seq[here, :].astype(jnp.float32)).astype(jnp.bfloat16)

    back_copies = []
    for hop in range(1, blocks):
        convolve(other_block(hop))
        copy = returning(hop)
        copy.start()
        back_copies.append(copy)
        send_queries(1)
    send_queries(PIECES)
    convolve(my_block)
    mixed_in[my_block] = mixed_out[lanes(my_block, block_rows), :]

    for copy in back_copies:
        copy.wait_recv()
    for index in range(PIECES):
        for copy in query_copies[index]:
            copy.wait_recv()
        for at in range(index * slab, (index + 1) * slab, columns):
            here = slice(at, at + columns)
            mixed = mixed_in[at // columns].astype(jnp.float32)
            product = query_rows[:, here].astype(jnp.float32) * mixed
            out_ref[:, here] = product.astype(jnp.bfloat16)
    query_copies = [copy for each in query_copies for copy in each]
    for copy in edge_copies + query_copies + seq_copies + back_copies:
        copy.wait_send()
    for copy in lags_copies + [halo_copy]:
        copy.wait_send()


def by_products(projected, short_taps, long_filter, skip_gain):
    chans = lax.axis_size("chan")
    blocks = lax.axis_size("ctx")
    my_block = lax.axis_index("ctx")
    own = projected[0].transpose(1, 0, 2)
    _, rows, channels = own.shape
    width = skip_gain.shape[0]
    columns = width // blocks
    groups, span = long_filter.shape[1], long_filter.shape[0]
    length = rows * chans * blocks
    gains = lax.dynamic_slice_in_dim(skip_gain, my_block * columns, columns, 0)[None]

    block_rows = rows * chans
    vmem = pl.BlockSpec(memory_space=pltpu.VMEM)
    dma = pltpu.SemaphoreType.DMA
    return pl.pallas_call(
        functools.partial(exchange_kernel, width // groups),
        out_shape=jax.ShapeDtypeStruct((block_rows, width), jnp.bfloat16),
        in_specs=[vmem] * 4,
        out_specs=vmem,
        scratch_shapes=[
            pltpu.VMEM((8, channels), jnp.float32),
            pltpu.VMEM((16, channels // 2), jnp.bfloat16),
            pltpu.VMEM((16, channels // 2), jnp.bfloat16),
            pltpu.VMEM((groups, span), jnp.float32),
            pltpu.VMEM((blocks, groups, span), jnp.float32),
            pltpu.VMEM((1, length + TILE), jnp.float32),
            pltpu.VMEM((rows, channels), jnp.bfloat16),
            pltpu.VMEM((rows, channels), jnp.bfloat16),
            pltpu.VMEM((block_rows, width), jnp.bfloat16),
            pltpu.VMEM((block_rows, width), jnp.bfloat16),
            pltpu.VMEM((length, columns), jnp.bfloat16),
            pltpu.VMEM((length, columns), jnp.bfloat16),
            pltpu.VMEM((blocks, block_rows, columns), jnp.bfloat16),
            pltpu.VMEM((block_rows, length), jnp.bfloat16),
            dma(()),
            dma(()),
            dma((blocks,)),
            dma((blocks,)),
            dma((2, chans)),
            dma((2, chans)),
            dma((PIECES, chans)),
            dma((PIECES, chans)),
            dma((chans, blocks)),
            dma((chans, blocks)),
            dma((blocks,)),
            dma((blocks,)),
        ],
        compiler_params=pltpu.CompilerParams(
            collective_id=0, has_side_effects=True, vmem_limit_bytes=48 * 1024 * 1024
        ),
    )(own, short_taps, long_filter.T, gains)


def local(projected, short_taps, long_filter, skip_gain):
    chans = lax.axis_size("chan")
    blocks = lax.axis_size("ctx")
    rows = projected.shape[1]
    width = skip_gain.shape[0]
    columns = width // blocks
    per_group = width // long_filter.shape[1]
    fits = columns % 128 == 0 and per_group % columns == 0
    fits = fits and rows % 32 == 0 and rows * chans % TILE == 0 and width % 256 == 0
    fits = fits and per_group % 128 == 0 and width // PIECES % columns == 0
    if fits:
        return by_products(projected, short_taps, long_filter, skip_gain)
    return by_transform(projected, short_taps, long_filter, skip_gain)


def solution(mesh):
    placed = (P("ctx", "chan", None, None), P(), P("ctx", "chan"), P("chan"))
    return jax.shard_map(
        local, mesh=mesh, in_specs=placed, out_specs=P("ctx", "chan"), check_vma=False
    )
```
